512 devices in a mesh: rec: 8 (over y, core), tm: 64 (over x, z).
Axes of the slice: x: 4, y: 4, z: 16, core: 2. Of those that a mesh axis runs over, the one named last changes fastest.
Arguments:
- summary: bfloat16 [8, 64, 1024, 1024], P('rec', 'tm'), as said below
- guess: bfloat16 [8, 16384, 1024], P('rec', 'tm'), may hold values from 0.099609375 to 3
- emission: bfloat16 [8, 16384, 1024], P('rec', 'tm'), may hold values from 0.049804688 to 1
- transition: bfloat16 [1024, 1024], P(None, 'rec'), as said below
- start: bfloat16 [8, 1024], P('rec'), may hold values from 0.099609375 to 3
Outputs:
- combined: bfloat16 [8, 32768, 1024], P('rec', 'tm')
- level_loglik: float32 [8], P('rec')
- forward: bfloat16 [8, 16384, 1024], P('rec', 'tm')
- frame_logscale: float32 [8, 16384], P('rec', 'tm')
The draws below stay inside these ranges and needn't reach their ends.
Inputs may be any that keep to these rules, and one draw needn't show every extreme that they name: `summary`: every entry is positive. `transition`: every entry is positive.
All inputs are finite; a program needn't handle non-finite values.
Results may differ from the reference program's by a relative error of at most 0.0052.
Values may be sent and summed in bfloat16 or wider, within the bound.
No kernel may reach another device: no remote copies, remote signals or barrier semaphores. Data moves between devices by JAX's collectives and lax.ppermute only.
A program may use at most 64 MiB of HBM per device.

```python
import math
import jax
import jax.numpy as jnp
from jax import lax

STATES = 1024
SWEEPS = 4
RECS = 8
BLOCKS = 64
PAIRS = 32
FRAMES = 16384


def draw_summary(key, part):
    key = jax.random.fold_in(key, 11)
    keys = jax.random.split(key, 5)
    shape = (RECS, BLOCKS, STATES, STATES)
    offdiag = jnp.exp(jax.random.uniform(keys[0], shape, jnp.float32, jnp.log(0.1), 0.0))
    row_scale = jnp.exp(jax.random.uniform(keys[2], (RECS, BLOCKS, STATES, 1), jnp.float32, 0.0, jnp.log(10.0)))
    trend_range = jnp.log(3.0)
    diag_value = 0.5 * STATES * jax.random.uniform(keys[1], (RECS, BLOCKS, STATES, 1), jnp.float32, 0.5, 1.5)
    col_scale = jnp.exp(jax.random.uniform(keys[3], (RECS, BLOCKS, 1, STATES), jnp.float32, 0.0, jnp.log(10.0)))
    block_scale = jnp.exp(jax.random.uniform(keys[4], (RECS, BLOCKS, 1, 1), jnp.float32, 0.0, jnp.log(1000.0)))
    row_ids = lax.broadcasted_iota(jnp.int32, (STATES, STATES), 0)
    col_ids = lax.broadcasted_iota(jnp.int32, (STATES, STATES), 1)
    block_factor = jnp.exp(trend_range * jnp.arange(BLOCKS, dtype=jnp.float32) / (BLOCKS - 1)).reshape(1, BLOCKS, 1, 1)
    matrix = jnp.where(row_ids == col_ids, diag_value, offdiag)
    return (matrix * (row_scale * col_scale * block_factor * block_scale / STATES)).astype(jnp.bfloat16)


def draw_transition(key, part):
    key = jax.random.fold_in(key, 23)
    keys = jax.random.split(key, 2)
    shape = (STATES, STATES)
    offdiag = jnp.exp(jax.random.uniform(keys[0], shape, jnp.float32, jnp.log(0.2), jnp.log(2.0)))
    diag_value = STATES * jax.random.uniform(keys[1], (STATES, 1), jnp.float32, 0.5, 1.5)
    row_ids = lax.broadcasted_iota(jnp.int32, shape, 0)
    col_ids = lax.broadcasted_iota(jnp.int32, shape, 1)
    return (jnp.where(row_ids == col_ids, diag_value, offdiag) / STATES).astype(jnp.bfloat16)


def level_of(stream_key, dims, cuts, least, high):
    gain = 1.0
    for axis_at, shards_of in cuts:
        heights = jax.random.uniform(jax.random.fold_in(jax.random.fold_in(stream_key, 6), axis_at), (shards_of,), jnp.float32, least / len(cuts), high / len(cuts))
        gain = gain * jnp.repeat(jnp.exp(heights), dims[axis_at] // shards_of).reshape((-1,) + (1,) * (len(dims) - 1 - axis_at))
    return gain


def setup_inputs(seed: int = 0) -> dict:
    arg_keys = jax.random.split(jax.random.key(seed), 6)
    summary = draw_summary(jax.random.fold_in(arg_keys[5], 71), 0)
    guess = jnp.clip(jnp.exp(math.log(3.0) - 3.4051113 * jax.random.uniform(arg_keys[1], (RECS, FRAMES, STATES), jnp.float32) ** level_of(arg_keys[1], (RECS, FRAMES, STATES), ((0, 8), (1, 64)), -0.2, 0.2)), 0.099609375, 3.0).astype(jnp.bfloat16)
    emission = jnp.clip(jnp.exp(math.log(1.0) - 2.9996462 * jax.random.uniform(arg_keys[2], (RECS, FRAMES, STATES), jnp.float32) ** level_of(arg_keys[2], (RECS, FRAMES, STATES), ((0, 8), (1, 64)), -0.2, 0.2)), 0.049804688, 1.0).astype(jnp.bfloat16)
    transition = draw_transition(jax.random.fold_in(arg_keys[5], 71), 0)
    start = jnp.clip(jnp.exp(math.log(3.0) - 3.4051113 * jax.random.uniform(arg_keys[4], (RECS, STATES), jnp.float32) ** level_of(arg_keys[4], (RECS, STATES), ((0, 8),), -0.2, 0.2)), 0.099609375, 3.0).astype(jnp.bfloat16)
    return dict(summary=summary, guess=guess, emission=emission, transition=transition, start=start)


def pair_product(tiles):
    product = jnp.dot(tiles[0], tiles[1], preferred_element_type=jnp.float32)
    pair_total = jnp.sum(product)
    combined = (product * (STATES * STATES / pair_total)).astype(jnp.bfloat16)
    return combined, pair_total


def reference(summary, guess, emission, transition, start):
    tiles = summary.reshape(RECS * PAIRS, 2, STATES, STATES)
    combined, totals = lax.map(pair_product, tiles)
    combined = combined.reshape(RECS, PAIRS * STATES, STATES)
    level_loglik = jnp.mean(jnp.log(totals.reshape(RECS, PAIRS) / STATES), axis=1)

    def sweeps(inputs):
        guess_rows, emission_rows, start_row = inputs
        forward_rows = guess_rows
        row_mean = jnp.ones((FRAMES, 1), jnp.float32)
        for sweep_index in range(SWEEPS):
            prior_rows = jnp.concatenate([start_row[None, :], forward_rows[:-1]], axis=0)
            unscaled = jnp.dot(prior_rows, transition, preferred_element_type=jnp.float32)
            unscaled = unscaled * emission_rows.astype(jnp.float32)
            row_mean = jnp.mean(unscaled, axis=1, keepdims=True)
            forward_rows = (unscaled / row_mean).astype(jnp.bfloat16)
        return forward_rows, jnp.log(row_mean[:, 0])

    forward, frame_logscale = lax.map(sweeps, (guess, emission, start))
    return combined, level_loglik, forward, frame_logscale
```

```python
import functools

import jax
import jax.numpy as jnp
from jax import lax
from jax.experimental import pallas as pl
from jax.experimental.pallas import tpu as pltpu
from jax.sharding import PartitionSpec as P

SWEEPS = 4
EDGE = 16
F32 = jnp.float32
BF16 = jnp.bfloat16
VMEM = pltpu.VMEM
HBM = pltpu.HBM
LIGHT = pl.CostEstimate(flops=1, bytes_accessed=1, transcendentals=0)


def parity():
    return lax.rem(lax.axis_index("tm"), 2)


def params(mib=24):
    return pltpu.CompilerParams(vmem_limit_bytes=mib * 1024 * 1024)


def matmul(a, b):
    return jnp.dot(a, b, preferred_element_type=F32)


def edge_kernel(sums, guess, emit, order, out):
    row = lax.broadcasted_iota(jnp.int32, out.shape, 0)
    rows = pltpu.roll(guess[...].astype(F32)[8:], 5, 0)
    out[...] = jnp.where(row == 0, sums[...], jnp.where(row < 5, rows, emit[...].astype(F32)[8:]))


def edge_after(sums, guess_rows, emit_rows, order):
    states = guess_rows.shape[1]
    last = guess_rows.shape[0] // EDGE - 1
    tail = pl.BlockSpec((EDGE, states), lambda i: (last, 0))
    return pl.pallas_call(
        edge_kernel,
        grid=(1,),
        in_specs=[pl.BlockSpec((1, states), lambda i: (0, 0)), tail, tail, pl.BlockSpec(memory_space=pl.ANY)],
        out_specs=pl.BlockSpec((8, states), lambda i: (0, 0)),
        out_shape=jax.ShapeDtypeStruct((8, states), F32),
        compiler_params=params(),
        cost_estimate=LIGHT,
        name="edge",
    )(sums, guess_rows, emit_rows, order)


def total_kernel(column_sums, row_sums, mine, logs, again):
    states = mine.shape[1]
    value = jnp.sum(column_sums[...] * row_sums[...], axis=1, keepdims=True)
    logs[...] = jnp.broadcast_to(jnp.log(value * (1.0 / states)), logs.shape)
    again[...] = mine[...]


def log_total(column_sums, row_sums, mine, peers):
    return pl.pallas_call(
        total_kernel,
        out_shape=(jax.ShapeDtypeStruct((peers, 128), F32), jax.ShapeDtypeStruct(mine.shape, F32)),
        compiler_params=params(),
        cost_estimate=LIGHT,
        name="log_total",
    )(column_sums, row_sums, mine)


def rows_kernel(first, tile, order, out):
    out[...] = tile[first:, :]


def rows_after(tile, first, order):
    rows, states = tile.shape
    return pl.pallas_call(
        functools.partial(rows_kernel, first),
        in_specs=[pl.BlockSpec(memory_space=VMEM), pl.BlockSpec(memory_space=pl.ANY)],
        out_shape=jax.ShapeDtypeStruct((rows - first, states), BF16),
        compiler_params=params(),
        cost_estimate=LIGHT,
        name="rows",
    )(tile, order)


def sweep_kernel(before, guess, emit, start, columns, others, order, out, logscale, held, table):
    blocks, states, width = columns.shape
    frames = guess.shape[0]
    first = lax.axis_index("tm") == 0
    edge = before[...]
    blank = jnp.zeros_like(edge)
    rows = frames + EDGE
    lead = SWEEPS
    prior = jnp.concatenate([blank, pltpu.roll(edge, 3, 0), guess[...].astype(F32)], axis=0)
    prior = pltpu.roll(prior, rows - (EDGE - lead), 0)
    emission = jnp.concatenate([blank, edge, emit[...].astype(F32)], axis=0)
    row = lax.broadcasted_iota(jnp.int32, (rows, 1), 0)
    start_row = start[...].astype(F32)
    held[...] = jnp.where(jnp.logical_and(first, row == lead - 1), start_row, prior).astype(BF16)
    core = lax.rem(lax.axis_index("rec"), 2)

    def fill(ref, place):
        for b in range(blocks):
            at = (2 * b + place) * width
            table[:, at : at + width] = ref[b]

    @pl.when(core == 0)
    def _():
        fill(columns, 0)
        fill(others, 1)

    @pl.when(core == 1)
    def _():
        fill(columns, 1)
        fill(others, 0)

    for m in range(1, SWEEPS + 1):
        now = rows if m < SWEEPS else frames
        shifted = pltpu.roll(emission, rows - (EDGE - lead + m), 0)[:now]
        unscaled = []
        for b in range(blocks):
            where = slice(2 * b * width, 2 * (b + 1) * width)
            unscaled.append(matmul(held[:now, :], table[:, where]) * shifted[:, where])
        mean = sum(jnp.sum(u, axis=1, keepdims=True) for u in unscaled) * (1.0 / states)
        inverse = 1.0 / mean
        for b, u in enumerate(unscaled):
            where = slice(2 * b * width, 2 * (b + 1) * width)
            scaled = u * inverse
            if m < SWEEPS:
                fixed = jnp.logical_and(first, row == lead - 1 - m)
                held[:, where] = jnp.where(fixed, start_row[:, where], scaled).astype(BF16)
            else:
                out[:, where] = scaled.astype(BF16)
        if m == SWEEPS:
            logscale[...] = jnp.transpose(jnp.broadcast_to(jnp.log(mean), (frames, 128)))[0:1, :]


def sweeps(before, guess, emit, start, columns, others, order):
    frames, states = guess.shape
    return pl.pallas_call(
        sweep_kernel,
        in_specs=[pl.BlockSpec(memory_space=VMEM)] * 6 + [pl.BlockSpec(memory_space=pl.ANY)],
        out_shape=(jax.ShapeDtypeStruct((frames, states), BF16), jax.ShapeDtypeStruct((1, frames), F32)),
        scratch_shapes=[VMEM((frames + EDGE, states), BF16), VMEM((states, states), BF16)],
        compiler_params=params(),
        cost_estimate=LIGHT,
        name="sweeps",
    )(before, guess, emit, start, columns, others, order)


def store_product(left, rights, scale, out, result, out_sems):
    parts, _, width = result.shape
    stores = []
    for p in range(parts):
        where = slice(p * width, (p + 1) * width)
        block = sum(matmul(left[:, first : first + ref.shape[0]], ref[:, where]) for first, ref in rights)
        result[p] = (block * scale).astype(BF16)
        stores.append(pltpu.make_async_copy(result.at[p], out.at[:, pl.ds(p * width, width)], out_sems.at[p]))
        stores[-1].start()
    for store in stores:
        store.wait()


def odd_kernel(own, lower, row_sums, before, out, result, out_sems):
    states = own.shape[0]

    @pl.when(parity() == 1)
    def _():
        scale = (states * states) / jnp.sum(row_sums[...] * before[0:1], axis=1, keepdims=True)
        store_product(lower[...], [(0, own)], scale, out, result, out_sems)


def even_kernel(own, got, column_sums, sums_got, other, order, out, result, out_sems):
    states = own.shape[0]

    @pl.when(parity() == 0)
    def _():
        scale = (states * states) / jnp.sum(column_sums[...] * sums_got[...], axis=1, keepdims=True)
        store_product(own[: states // 2, :], [(0, got)], scale, out, result, out_sems)


def product_call(kernel, name, cost, operands, aliased=None, order=()):
    states = operands[0].shape[0]
    half, parts = states // 2, 4
    specs = [pl.BlockSpec(memory_space=VMEM)] * len(operands)
    if aliased is not None:
        specs.append(pl.BlockSpec(memory_space=HBM))
        operands = operands + [aliased]
    return pl.pallas_call(
        kernel,
        in_specs=specs + [pl.BlockSpec(memory_space=pl.ANY)] * len(order),
        out_specs=pl.BlockSpec(memory_space=HBM),
        out_shape=jax.ShapeDtypeStruct((half, states), BF16),
        scratch_shapes=[VMEM((parts, half, states // parts), BF16), pltpu.SemaphoreType.DMA((parts,))],
        input_output_aliases={} if aliased is None else {len(operands) - 1: 0},
        compiler_params=params(),
        cost_estimate=cost,
        name=name,
    )(*operands, *order)


def mean_kernel(logs, order, level):
    level[...] = jnp.sum(logs[...], axis=0, keepdims=True) * (1.0 / logs.shape[0])


def mean_after(logs, order):
    return pl.pallas_call(
        mean_kernel,
        in_specs=[pl.BlockSpec(memory_space=VMEM), pl.BlockSpec(memory_space=pl.ANY)],
        out_shape=jax.ShapeDtypeStruct((1, 128), F32),
        compiler_params=params(),
        cost_estimate=LIGHT,
        name="mean_log",
    )(logs, order)


def local(summary, guess, emission, transition, start):
    tile = summary[0, 0]
    states = tile.shape[0]
    size, recs = lax.axis_size("tm"), lax.axis_size("rec")
    even = lax.axis_index("tm") % 2 == 0
    back = [(t, t - 1) for t in range(1, size, 2)]
    over = [(t, t + 1) for t in range(0, size, 2)]
    planes = size // 4
    peers = [[r * size + t for t in range(0, size, 2)] for r in range(recs)]
    peers += [[r * size + t for r in range(recs) for t in range(z, size, planes)] for z in range(1, planes, 2)]
    cores = [list(range(c, recs, 2)) for c in range(2)]

    got = lax.ppermute(tile, "tm", back)
    copies = jnp.broadcast_to(transition[None], (recs // 2,) + transition.shape)
    columns = lax.all_to_all(copies, "rec", 0, 0, tiled=True, axis_index_groups=cores)
    wide = tile.astype(F32)
    column_sums, row_sums = jnp.sum(wide, axis=0)[None], jnp.sum(wide, axis=1)[None]
    pair_columns = lax.ppermute(column_sums, "tm", [(t, (t + 2) % size) for t in range(0, size, 2)])
    pair_rows = lax.ppermute(row_sums, "tm", [(t, (t + 1) % size) for t in range(1, size, 2)])
    logs, row_sums_again = log_total(pair_columns, pair_rows, row_sums, size // 2)
    lower = lax.ppermute(rows_after(tile, states // 2, logs), "tm", over)
    all_logs = lax.all_to_all(logs, ("rec", "tm"), 0, 0, tiled=True, axis_index_groups=peers)
    others = lax.ppermute(columns, "rec", [(r, r ^ 1) for r in range(recs)])
    edge = edge_after(column_sums, guess[0], emission[0], logs)
    before = lax.ppermute(edge, "tm", [(t, t + 1) for t in range(size - 1)])
    combined = product_call(odd_kernel, "odd_product", LIGHT, [tile, lower, row_sums, before])
    forward, frame_logscale = sweeps(before, guess[0], emission[0], start, columns, others, combined)
    level = mean_after(all_logs, frame_logscale)[0, :1]
    told = lax.ppermute(level, "tm", over)
    sums_got = lax.ppermute(row_sums_again, "tm", back)
    combined = product_call(
        even_kernel, "even_product", LIGHT, [tile, got, column_sums, sums_got], combined, (frame_logscale,)
    )
    return combined[None], jnp.where(even, level, told), forward[None], frame_logscale


def solution(mesh):
    return jax.shard_map(
        local,
        mesh=mesh,
        in_specs=(
            P("rec", "tm", None, None),
            P("rec", "tm", None),
            P("rec", "tm", None),
            P(None, "rec"),
            P("rec", None),
        ),
        out_specs=(P("rec", "tm", None), P("rec"), P("rec", "tm", None), P("rec", "tm")),
        check_vma=False,
    )
```

```python
import functools

import jax
import jax.numpy as jnp
from jax import lax
from jax.experimental import pallas as pl
from jax.experimental.pallas import tpu as pltpu
from jax.sharding import PartitionSpec as P

SWEEPS = 4
EDGE = 16
F32 = jnp.float32
BF16 = jnp.bfloat16
VMEM = pltpu.VMEM
HBM = pltpu.HBM
TOTAL_COST = pl.CostEstimate(flops=12 * 10**9, bytes_accessed=24 * 10**6, transcendentals=0)
LIGHT = pl.CostEstimate(flops=1, bytes_accessed=1, transcendentals=0)


def parity():
    return lax.rem(lax.axis_index("tm"), 2)


def params(mib=24):
    return pltpu.CompilerParams(vmem_limit_bytes=mib * 1024 * 1024)


def matmul(a, b):
    return jnp.dot(a, b, preferred_element_type=F32)


def edge_kernel(column_sums, row_sums, guess, emit, out):
    row = lax.broadcasted_iota(jnp.int32, out.shape, 0)
    sums = jnp.where(parity() == 0, column_sums[...], row_sums[...])
    rows = pltpu.roll(guess[...].astype(F32)[8:], 5, 0)
    out[...] = jnp.where(row == 0, sums, jnp.where(row < 5, rows, emit[...].astype(F32)[8:]))


def make_edge(column_sums, row_sums, guess_rows, emit_rows):
    states = guess_rows.shape[1]
    last = guess_rows.shape[0] // EDGE - 1
    tail = pl.BlockSpec((EDGE, states), lambda i: (last, 0))
    return pl.pallas_call(
        edge_kernel,
        grid=(1,),
        in_specs=[pl.BlockSpec((1, states), lambda i: (0, 0))] * 2 + [tail, tail],
        out_specs=pl.BlockSpec((8, states), lambda i: (0, 0)),
        out_shape=jax.ShapeDtypeStruct((8, states), F32),
        compiler_params=params(),
        cost_estimate=LIGHT,
        name="edge",
    )(column_sums, row_sums, guess_rows, emit_rows)


def total_kernel(column_sums, before, order, totals):
    value = jnp.sum(column_sums[...] * before[0:1], axis=1, keepdims=True)
    totals[...] = jnp.broadcast_to(value, totals.shape)


def pair_total(column_sums, before, peers, order):
    return pl.pallas_call(
        total_kernel,
        in_specs=[pl.BlockSpec(memory_space=VMEM)] * 2 + [pl.BlockSpec(memory_space=pl.ANY)],
        out_shape=jax.ShapeDtypeStruct((peers, 128), F32),
        compiler_params=params(),
        cost_estimate=TOTAL_COST,
        name="pair_total",
    )(column_sums, before, order)


def copies_kernel(shard, out):
    for c in range(out.shape[0]):
        out[c] = shard[...]


def copies_of(shard, count):
    return pl.pallas_call(
        copies_kernel,
        out_shape=jax.ShapeDtypeStruct((count,) + shard.shape, BF16),
        compiler_params=params(),
        cost_estimate=LIGHT,
        name="copies",
    )(shard)


def sweep_kernel(
    before, start, guess_in, emit_in, columns, others, out, logscale, token, guess, emit, held, table, row_sems, sems
):
    blocks, states, width = columns.shape
    frames = guess.shape[0]
    first = lax.axis_index("tm") == 0
    core = lax.rem(lax.axis_index("rec"), 2)

    def table_loads(mine):
        copies = []
        for b in range(blocks):
            for k, ref in enumerate((columns, others)):
                at = (2 * b + (mine if k == 0 else 1 - mine)) * width
                copies.append(pltpu.make_async_copy(ref.at[b], table.at[:, pl.ds(at, width)], sems.at[2 * b + k]))
        return copies

    row_loads = [
        pltpu.make_async_copy(guess_in, guess, row_sems.at[0]),
        pltpu.make_async_copy(emit_in, emit, row_sems.at[1]),
    ]
    for copy in row_loads:
        copy.start()
    for mine in range(2):

        @pl.when(core == mine)
        def _():
            for copy in table_loads(mine):
                copy.start()

    for copy in row_loads:
        copy.wait()
    edge = before[...]
    blank = jnp.zeros_like(edge)
    rows = frames + EDGE
    lead = SWEEPS
    prior = jnp.concatenate([blank, pltpu.roll(edge, 3, 0), guess[...].astype(F32)], axis=0)
    prior = pltpu.roll(prior, rows - (EDGE - lead), 0)
    emission = jnp.concatenate([blank, edge, emit[...].astype(F32)], axis=0)
    row = lax.broadcasted_iota(jnp.int32, (rows, 1), 0)
    start_row = start[...].astype(F32)
    held[...] = jnp.where(jnp.logical_and(first, row == lead - 1), start_row, prior).astype(BF16)
    for copy in table_loads(0):
        copy.wait()
    for m in range(1, SWEEPS + 1):
        now = rows if m < SWEEPS else frames
        shifted = pltpu.roll(emission, rows - (EDGE - lead + m), 0)[:now]
        unscaled = []
        for b in range(blocks):
            where = slice(2 * b * width, 2 * (b + 1) * width)
            unscaled.append(matmul(held[:now, :], table[:, where]) * shifted[:, where])
        lanes = sum(u[:, :128] + u[:, 128:] for u in unscaled)
        mean = jnp.sum(lanes, axis=1, keepdims=True) * (1.0 / states)
        inverse = 1.0 / mean
        for b, u in enumerate(unscaled):
            where = slice(2 * b * width, 2 * (b + 1) * width)
            scaled = u * inverse
            if m < SWEEPS:
                fixed = jnp.logical_and(first, row == lead - 1 - m)
                held[:, where] = jnp.where(fixed, start_row[:, where], scaled).astype(BF16)
            else:
                out[:, where] = scaled.astype(BF16)
        if m == SWEEPS:
            logscale[...] = jnp.transpose(jnp.broadcast_to(jnp.log(mean), (frames, 128)))[0:1, :]
    token[...] = jnp.zeros_like(token)


def sweeps(before, guess, emit, start, columns, others):
    frames, states = guess.shape
    return pl.pallas_call(
        sweep_kernel,
        in_specs=[pl.BlockSpec(memory_space=VMEM)] * 2 + [pl.BlockSpec(memory_space=pl.ANY)] * 4,
        out_shape=(
            jax.ShapeDtypeStruct((frames, states), BF16),
            jax.ShapeDtypeStruct((1, frames), F32),
            jax.ShapeDtypeStruct((8, 128), F32),
        ),
        scratch_shapes=[
            VMEM((frames, states), BF16),
            VMEM((frames, states), BF16),
            VMEM((frames + EDGE, states), BF16),
            VMEM((states, states), BF16),
            pltpu.SemaphoreType.DMA((2,)),
            pltpu.SemaphoreType.DMA((2 * columns.shape[0],)),
        ],
        compiler_params=params(),
        cost_estimate=LIGHT,
        name="sweeps",
    )(before, start, guess, emit, columns, others)


def product_kernel(
    own, lower, got, column_sums, sums_got, row_sums, before, order, out, token, right, total, result, load_sems, out_sems
):
    states = own.shape[0]
    parts, depth, _ = right.shape
    half = states // 2
    even = parity() == 0
    token[...] = jnp.zeros_like(token)

    def store(p):
        rows = pl.ds(p * (half // parts), half // parts)
        return pltpu.make_async_copy(result.at[rows, :], out.at[rows, :], out_sems.at[p])

    def finish(scale):
        for p in range(parts):
            rows = slice(p * (half // parts), (p + 1) * (half // parts))
            result[rows, :] = (total[rows, :] * scale).astype(BF16)
            store(p).start()

    @pl.when(even)
    def _():
        loads = [
            pltpu.make_async_copy(got.at[pl.ds(p * depth, depth), :], right.at[p], load_sems.at[p]) for p in range(parts)
        ]
        for load in loads:
            load.start()
        scale = (states * states) / jnp.sum(column_sums[...] * sums_got[...], axis=1, keepdims=True)
        for p in range(parts):
            loads[p].wait()
            block = matmul(own[:half, p * depth : (p + 1) * depth], right[p])
            total[...] = block if p == 0 else total[...] + block
        finish(scale)

    @pl.when(jnp.logical_not(even))
    def _():
        scale = (states * states) / jnp.sum(row_sums[...] * before[0:1], axis=1, keepdims=True)
        total[...] = matmul(lower[...], own[...])
        finish(scale)

    for p in range(parts):
        store(p).wait()


def pair_product(own, lower, got, column_sums, sums_got, row_sums, before, order):
    states = own.shape[0]
    half, parts = states // 2, 4
    spaces = (VMEM, VMEM, pl.ANY, VMEM, VMEM, VMEM, VMEM, pl.ANY)
    return pl.pallas_call(
        product_kernel,
        in_specs=[pl.BlockSpec(memory_space=space) for space in spaces],
        out_specs=[pl.BlockSpec(memory_space=HBM), pl.BlockSpec(memory_space=VMEM)],
        out_shape=(jax.ShapeDtypeStruct((half, states), BF16), jax.ShapeDtypeStruct((8, 128), F32)),
        scratch_shapes=[
            VMEM((parts, states // parts, states), BF16),
            VMEM((half, states), F32),
            VMEM((half, states), BF16),
            pltpu.SemaphoreType.DMA((parts,)),
            pltpu.SemaphoreType.DMA((parts,)),
        ],
        compiler_params=params(),
        cost_estimate=LIGHT,
        name="pair_product",
    )(own, lower, got, column_sums, sums_got, row_sums, before, order)


def mean_kernel(states, totals, order, level):
    logs = jnp.log(totals[...] * (1.0 / states))
    level[...] = jnp.sum(logs, axis=0, keepdims=True) * (1.0 / logs.shape[0])


def mean_log(totals, states, order):
    return pl.pallas_call(
        functools.partial(mean_kernel, states),
        in_specs=[pl.BlockSpec(memory_space=VMEM), pl.BlockSpec(memory_space=pl.ANY)],
        out_shape=jax.ShapeDtypeStruct((1, 128), F32),
        compiler_params=params(),
        cost_estimate=LIGHT,
        name="mean_log",
    )(totals, order)


def local(summary, guess, emission, transition, start):
    tile = summary[0, 0]
    states = tile.shape[0]
    size, recs = lax.axis_size("tm"), lax.axis_size("rec")
    even = lax.axis_index("tm") % 2 == 0
    back = [(t, t - 1) for t in range(1, size, 2)]
    over = [(t, t + 1) for t in range(0, size, 2)]
    planes = size // 4
    peers = [[r * size + t for t in range(0, size, 2)] for r in range(recs)]
    peers += [[r * size + t for r in range(recs) for t in range(z, size, planes)] for z in range(1, planes, 2)]
    cores = [list(range(c, recs, 2)) for c in range(2)]

    got = lax.ppermute(tile, "tm", back)
    copies = copies_of(transition, recs // 2)
    columns = lax.all_to_all(copies, "rec", 0, 0, tiled=True, axis_index_groups=cores)
    wide = tile.astype(F32)
    column_sums, row_sums = jnp.sum(wide, axis=0)[None], jnp.sum(wide, axis=1)[None]
    pair_columns = lax.ppermute(column_sums, "tm", [(t, (t + 2) % size) for t in range(0, size, 2)])
    edge = make_edge(column_sums, row_sums, guess[0], emission[0])
    before = lax.ppermute(edge, "tm", [(t, (t + 1) % size) for t in range(size)])
    lower = lax.ppermute(tile[states // 2 :], "tm", over)
    totals = pair_total(pair_columns, before, size // 2, lower)
    totals = lax.all_to_all(totals, ("rec", "tm"), 0, 0, tiled=True, axis_index_groups=peers)
    others = lax.ppermute(columns, "rec", [(r, r ^ 1) for r in range(recs)])
    sums_got = lax.ppermute(row_sums, "tm", back)
    forward, frame_logscale, token = sweeps(before, guess[0], emission[0], start, columns, others)
    combined, token = pair_product(tile, lower, got, column_sums, sums_got, row_sums, before, token)
    level = mean_log(totals, states, token)[0, :1]
    told = lax.ppermute(level, "tm", over)
    return combined[None], jnp.where(even, level, told), forward[None], frame_logscale


def solution(mesh):
    return jax.shard_map(
        local,
        mesh=mesh,
        in_specs=(
            P("rec", "tm", None, None),
            P("rec", "tm", None),
            P("rec", "tm", None),
            P(None, "rec"),
            P("rec", None),
        ),
        out_specs=(P("rec", "tm", None), P("rec"), P("rec", "tm", None), P("rec", "tm")),
        check_vma=False,
    )
```

```python
import functools

import jax
import jax.numpy as jnp
from jax import lax
from jax.experimental import pallas as pl
from jax.experimental.pallas import tpu as pltpu
from jax.sharding import PartitionSpec as P

SWEEPS = 4
EDGE = 16
F32 = jnp.float32
BF16 = jnp.bfloat16
VMEM = pltpu.VMEM
HBM = pltpu.HBM
SPREAD_COST = pl.CostEstimate(flops=12 * 10**9, bytes_accessed=24 * 10**6, transcendentals=0)
LIGHT = pl.CostEstimate(flops=1, bytes_accessed=1, transcendentals=0)


def parity():
    return lax.rem(lax.axis_index("tm"), 2)


def params(mib=24):
    return pltpu.CompilerParams(vmem_limit_bytes=mib * 1024 * 1024)


def matmul(a, b):
    return jnp.dot(a, b, preferred_element_type=F32)


def edge_kernel(column_sums, guess, emit, out):
    row = lax.broadcasted_iota(jnp.int32, out.shape, 0)
    rows = pltpu.roll(guess[...].astype(F32)[8:], 5, 0)
    out[...] = jnp.where(row == 0, column_sums[...], jnp.where(row < 5, rows, emit[...].astype(F32)[8:]))


def make_edge(column_sums, guess_rows, emit_rows):
    states = guess_rows.shape[1]
    last = guess_rows.shape[0] // EDGE - 1
    tail = pl.BlockSpec((EDGE, states), lambda i: (last, 0))
    return pl.pallas_call(
        edge_kernel,
        grid=(1,),
        in_specs=[pl.BlockSpec((1, states), lambda i: (0, 0)), tail, tail],
        out_specs=pl.BlockSpec((8, states), lambda i: (0, 0)),
        out_shape=jax.ShapeDtypeStruct((8, states), F32),
        compiler_params=params(),
        cost_estimate=LIGHT,
        name="edge",
    )(column_sums, guess_rows, emit_rows)


def total_kernel(before, row_sums, total):
    value = jnp.sum(before[0:1] * row_sums[...], axis=1, keepdims=True)
    total[...] = jnp.broadcast_to(value, total.shape)


def pair_total(before, row_sums):
    return pl.pallas_call(
        total_kernel,
        out_shape=jax.ShapeDtypeStruct((8, 128), F32),
        compiler_params=params(),
        cost_estimate=LIGHT,
        name="pair_total",
    )(before, row_sums)


def spread_kernel(total, out):
    out[...] = jnp.broadcast_to(total[0:1, :], out.shape)


def spread(total, peers):
    return pl.pallas_call(
        spread_kernel,
        out_shape=jax.ShapeDtypeStruct((peers, 128), F32),
        compiler_params=params(),
        cost_estimate=SPREAD_COST,
        name="spread",
    )(total)


def copies_kernel(shard, out):
    for c in range(out.shape[0]):
        out[c] = shard[...]


def copies_of(shard, count):
    return pl.pallas_call(
        copies_kernel,
        out_shape=jax.ShapeDtypeStruct((count,) + shard.shape, BF16),
        compiler_params=params(),
        cost_estimate=LIGHT,
        name="copies",
    )(shard)


def rows_kernel(first, tile, *refs):
    refs[-1][...] = tile[first:, :]


def rows_after(tile, first, *order):
    rows, states = tile.shape
    return pl.pallas_call(
        functools.partial(rows_kernel, first),
        in_specs=[pl.BlockSpec(memory_space=VMEM)] + [pl.BlockSpec(memory_space=pl.ANY)] * len(order),
        out_shape=jax.ShapeDtypeStruct((rows - first, states), BF16),
        compiler_params=params(),
        cost_estimate=LIGHT,
        name="rows",
    )(tile, *order)


def sweep_kernel(
    before, start, guess_in, emit_in, columns, others, out, logscale, token, guess, emit, held, table, row_sems, sems
):
    blocks, states, width = columns.shape
    frames = guess.shape[0]
    first = lax.axis_index("tm") == 0
    core = lax.rem(lax.axis_index("rec"), 2)

    def table_loads(mine):
        copies = []
        for b in range(blocks):
            for k, ref in enumerate((columns, others)):
                at = (2 * b + (mine if k == 0 else 1 - mine)) * width
                copies.append(pltpu.make_async_copy(ref.at[b], table.at[:, pl.ds(at, width)], sems.at[2 * b + k]))
        return copies

    row_loads = [
        pltpu.make_async_copy(guess_in, guess, row_sems.at[0]),
        pltpu.make_async_copy(emit_in, emit, row_sems.at[1]),
    ]
    for copy in row_loads:
        copy.start()
    for mine in range(2):

        @pl.when(core == mine)
        def _():
            for copy in table_loads(mine):
                copy.start()

    for copy in row_loads:
        copy.wait()
    edge = before[...]
    blank = jnp.zeros_like(edge)
    rows = frames + EDGE
    lead = SWEEPS
    prior = jnp.concatenate([blank, pltpu.roll(edge, 3, 0), guess[...].astype(F32)], axis=0)
    prior = pltpu.roll(prior, rows - (EDGE - lead), 0)
    emission = jnp.concatenate([blank, edge, emit[...].astype(F32)], axis=0)
    row = lax.broadcasted_iota(jnp.int32, (rows, 1), 0)
    start_row = start[...].astype(F32)
    held[...] = jnp.where(jnp.logical_and(first, row == lead - 1), start_row, prior).astype(BF16)
    for copy in table_loads(0):
        copy.wait()
    for m in range(1, SWEEPS + 1):
        now = rows if m < SWEEPS else frames
        shifted = pltpu.roll(emission, rows - (EDGE - lead + m), 0)[:now]
        unscaled = []
        for b in range(blocks):
            where = slice(2 * b * width, 2 * (b + 1) * width)
            unscaled.append(matmul(held[:now, :], table[:, where]) * shifted[:, where])
        lanes = sum(u[:, :128] + u[:, 128:] for u in unscaled)
        mean = jnp.sum(lanes, axis=1, keepdims=True) * (1.0 / states)
        inverse = 1.0 / mean
        for b, u in enumerate(unscaled):
            where = slice(2 * b * width, 2 * (b + 1) * width)
            scaled = u * inverse
            if m < SWEEPS:
                fixed = jnp.logical_and(first, row == lead - 1 - m)
                held[:, where] = jnp.where(fixed, start_row[:, where], scaled).astype(BF16)
            else:
                out[:, where] = scaled.astype(BF16)
        if m == SWEEPS:
            logscale[...] = jnp.transpose(jnp.broadcast_to(jnp.log(mean), (frames, 128)))[0:1, :]
    token[...] = jnp.zeros_like(token)


def sweeps(before, guess, emit, start, columns, others):
    frames, states = guess.shape
    return pl.pallas_call(
        sweep_kernel,
        in_specs=[pl.BlockSpec(memory_space=VMEM)] * 2 + [pl.BlockSpec(memory_space=pl.ANY)] * 4,
        out_shape=(
            jax.ShapeDtypeStruct((frames, states), BF16),
            jax.ShapeDtypeStruct((1, frames), F32),
            jax.ShapeDtypeStruct((8, 128), F32),
        ),
        scratch_shapes=[
            VMEM((frames, states), BF16),
            VMEM((frames, states), BF16),
            VMEM((frames + EDGE, states), BF16),
            VMEM((states, states), BF16),
            pltpu.SemaphoreType.DMA((2,)),
            pltpu.SemaphoreType.DMA((2 * columns.shape[0],)),
        ],
        compiler_params=params(),
        cost_estimate=LIGHT,
        name="sweeps",
    )(before, start, guess, emit, columns, others)


def product_kernel(
    own, column_sums, row_sums, before, lower, got, order, out, token, right, left, total, result, load_sems, out_sems
):
    states = own.shape[0]
    parts, depth, _ = right.shape
    half = states // 2
    even = parity() == 0
    token[...] = jnp.zeros_like(token)

    def store(p):
        rows = pl.ds(p * (half // parts), half // parts)
        return pltpu.make_async_copy(result.at[rows, :], out.at[rows, :], out_sems.at[p])

    def finish(scale):
        for p in range(parts):
            rows = slice(p * (half // parts), (p + 1) * (half // parts))
            result[rows, :] = (total[rows, :] * scale).astype(BF16)
            store(p).start()

    @pl.when(even)
    def _():
        loads = [
            pltpu.make_async_copy(got.at[pl.ds(p * depth, depth), :], right.at[p], load_sems.at[p]) for p in range(parts)
        ]
        for load in loads:
            load.start()
        sums = column_sums[...]
        high = sums.astype(BF16).astype(F32)
        mid = (sums - high).astype(BF16).astype(F32)
        row = lax.broadcasted_iota(jnp.int32, (EDGE, states), 0)
        low = sums - high - mid
        split = jnp.where(row == 0, high, jnp.where(row == 1, mid, jnp.where(row == 2, low, 0.0))).astype(BF16)
        for p in range(parts):
            where = slice(p * depth, (p + 1) * depth)
            loads[p].wait()
            block = matmul(jnp.concatenate([own[:half, where], split[:, where]], axis=0), right[p])
            total[...] = block if p == 0 else total[...] + block
        pair = jnp.sum(jnp.sum(total[half:, :], axis=0, keepdims=True), axis=1, keepdims=True)
        finish((states * states) / pair)

    @pl.when(jnp.logical_not(even))
    def _():
        load = pltpu.make_async_copy(lower, left, load_sems.at[0])
        load.start()
        scale = (states * states) / jnp.sum(row_sums[...] * before[0:1], axis=1, keepdims=True)
        load.wait()
        total[:half, :] = matmul(left[...], own[...])
        finish(scale)

    for p in range(parts):
        store(p).wait()


def pair_product(own, column_sums, row_sums, before, lower, got, order):
    states = own.shape[0]
    half, parts = states // 2, 4
    return pl.pallas_call(
        product_kernel,
        in_specs=[pl.BlockSpec(memory_space=VMEM)] * 4 + [pl.BlockSpec(memory_space=pl.ANY)] * 3,
        out_specs=[pl.BlockSpec(memory_space=HBM), pl.BlockSpec(memory_space=VMEM)],
        out_shape=(jax.ShapeDtypeStruct((half, states), BF16), jax.ShapeDtypeStruct((8, 128), F32)),
        scratch_shapes=[
            VMEM((parts, states // parts, states), BF16),
            VMEM((half, states), BF16),
            VMEM((half + EDGE, states), F32),
            VMEM((half, states), BF16),
            pltpu.SemaphoreType.DMA((parts,)),
            pltpu.SemaphoreType.DMA((parts,)),
        ],
        compiler_params=params(),
        cost_estimate=LIGHT,
        name="pair_product",
    )(own, column_sums, row_sums, before, lower, got, order)


def mean_kernel(states, totals, order, level):
    logs = jnp.log(totals[...] * (1.0 / states))
    level[...] = jnp.sum(logs, axis=0, keepdims=True) * (1.0 / logs.shape[0])


def mean_log(totals, states, order):
    return pl.pallas_call(
        functools.partial(mean_kernel, states),
        in_specs=[pl.BlockSpec(memory_space=VMEM), pl.BlockSpec(memory_space=pl.ANY)],
        out_shape=jax.ShapeDtypeStruct((1, 128), F32),
        compiler_params=params(),
        cost_estimate=LIGHT,
        name="mean_log",
    )(totals, order)


def local(summary, guess, emission, transition, start):
    tile = summary[0, 0]
    states = tile.shape[0]
    size, recs = lax.axis_size("tm"), lax.axis_size("rec")
    even = lax.axis_index("tm") % 2 == 0
    back = [(t, t - 1) for t in range(1, size, 2)]
    over = [(t, t + 1) for t in range(0, size, 2)]
    planes = size // 4
    peers = [[r * size + t for t in range(0, size, 2)] for r in range(recs)]
    peers += [[r * size + t for r in range(recs) for t in range(z, size, planes)] for z in range(1, planes, 2)]
    cores = [list(range(c, recs, 2)) for c in range(2)]

    got = lax.ppermute(tile, "tm", back)
    copies = copies_of(transition, recs // 2)
    columns = lax.all_to_all(copies, "rec", 0, 0, tiled=True, axis_index_groups=cores)
    wide = tile.astype(F32)
    column_sums, row_sums = jnp.sum(wide, axis=0)[None], jnp.sum(wide, axis=1)[None]
    edge = make_edge(column_sums, guess[0], emission[0])
    before = lax.ppermute(edge, "tm", [(t, (t + 1) % size) for t in range(size)])
    lower = lax.ppermute(rows_after(tile, states // 2, before), "tm", over)
    total = lax.ppermute(pair_total(before, row_sums), "tm", [(t, (t + 1) % size) for t in range(1, size, 2)])
    totals = spread(total, size // 2)
    totals = lax.all_to_all(totals, ("rec", "tm"), 0, 0, tiled=True, axis_index_groups=peers)
    others = lax.ppermute(columns, "rec", [(r, r ^ 1) for r in range(recs)])
    forward, frame_logscale, token = sweeps(before, guess[0], emission[0], start, columns, others)
    combined, token = pair_product(tile, column_sums, row_sums, before, lower, got, token)
    level = mean_log(totals, states, token)[0, :1]
    told = lax.ppermute(level, "tm", over)
    return combined[None], jnp.where(even, level, told), forward[None], frame_logscale


def solution(mesh):
    return jax.shard_map(
        local,
        mesh=mesh,
        in_specs=(
            P("rec", "tm", None, None),
            P("rec", "tm", None),
            P("rec", "tm", None),
            P(None, "rec"),
            P("rec", None),
        ),
        out_specs=(P("rec", "tm", None), P("rec"), P("rec", "tm", None), P("rec", "tm")),
        check_vma=False,
    )
```

```python
import functools

import jax
import jax.numpy as jnp
from jax import lax
from jax.experimental import pallas as pl
from jax.experimental.pallas import tpu as pltpu
from jax.sharding import PartitionSpec as P

SWEEPS = 4
EDGE = 16
F32 = jnp.float32
BF16 = jnp.bfloat16
VMEM = pltpu.VMEM
HBM = pltpu.HBM
SPREAD_COST = pl.CostEstimate(flops=12 * 10**9, bytes_accessed=24 * 10**6, transcendentals=0)
LIGHT = pl.CostEstimate(flops=1, bytes_accessed=1, transcendentals=0)


def parity():
    return lax.rem(lax.axis_index("tm"), 2)


def params(mib=24):
    return pltpu.CompilerParams(vmem_limit_bytes=mib * 1024 * 1024)


def matmul(a, b):
    return jnp.dot(a, b, preferred_element_type=F32)


def edge_kernel(column_sums, guess, emit, out):
    row = lax.broadcasted_iota(jnp.int32, out.shape, 0)
    rows = pltpu.roll(guess[...].astype(F32)[8:], 5, 0)
    out[...] = jnp.where(row == 0, column_sums[...], jnp.where(row < 5, rows, emit[...].astype(F32)[8:]))


def make_edge(column_sums, guess_rows, emit_rows):
    states = guess_rows.shape[1]
    last = guess_rows.shape[0] // EDGE - 1
    tail = pl.BlockSpec((EDGE, states), lambda i: (last, 0))
    return pl.pallas_call(
        edge_kernel,
        grid=(1,),
        in_specs=[pl.BlockSpec((1, states), lambda i: (0, 0)), tail, tail],
        out_specs=pl.BlockSpec((8, states), lambda i: (0, 0)),
        out_shape=jax.ShapeDtypeStruct((8, states), F32),
        compiler_params=params(),
        cost_estimate=LIGHT,
        name="edge",
    )(column_sums, guess_rows, emit_rows)


def total_kernel(before, row_sums, total):
    value = jnp.sum(before[0:1] * row_sums[...], axis=1, keepdims=True)
    total[...] = jnp.broadcast_to(value, total.shape)


def pair_total(before, row_sums):
    return pl.pallas_call(
        total_kernel,
        out_shape=jax.ShapeDtypeStruct((8, 128), F32),
        compiler_params=params(),
        cost_estimate=LIGHT,
        name="pair_total",
    )(before, row_sums)


def spread_kernel(total, out):
    out[...] = jnp.broadcast_to(total[0:1, :], out.shape)


def spread(total, peers):
    return pl.pallas_call(
        spread_kernel,
        out_shape=jax.ShapeDtypeStruct((peers, 128), F32),
        compiler_params=params(),
        cost_estimate=SPREAD_COST,
        name="spread",
    )(total)


def copies_kernel(shard, out):
    for c in range(out.shape[0]):
        out[c] = shard[...]


def copies_of(shard, count):
    return pl.pallas_call(
        copies_kernel,
        out_shape=jax.ShapeDtypeStruct((count,) + shard.shape, BF16),
        compiler_params=params(),
        cost_estimate=LIGHT,
        name="copies",
    )(shard)


def rows_kernel(tile, order, out, held, sems, out_sems):
    parts, rows, _ = held.shape
    first = tile.shape[0] - parts * rows
    loads = [
        pltpu.make_async_copy(tile.at[pl.ds(first + p * rows, rows), :], held.at[p], sems.at[p]) for p in range(parts)
    ]
    stores = [pltpu.make_async_copy(held.at[p], out.at[pl.ds(p * rows, rows), :], out_sems.at[p]) for p in range(parts)]

    @pl.when(parity() == 0)
    def _():
        for load in loads:
            load.start()
        for load, store in zip(loads, stores):
            load.wait()
            store.start()
        for store in stores:
            store.wait()


def rows_after(tile, first, order):
    rows, states = tile.shape[0] - first, tile.shape[1]
    parts = 4
    return pl.pallas_call(
        rows_kernel,
        in_specs=[pl.BlockSpec(memory_space=HBM), pl.BlockSpec(memory_space=pl.ANY)],
        out_specs=pl.BlockSpec(memory_space=HBM),
        out_shape=jax.ShapeDtypeStruct((rows, states), BF16),
        scratch_shapes=[
            VMEM((parts, rows // parts, states), BF16),
            pltpu.SemaphoreType.DMA((parts,)),
            pltpu.SemaphoreType.DMA((parts,)),
        ],
        compiler_params=params(),
        cost_estimate=LIGHT,
        name="rows",
    )(tile, order)


def sweep_kernel(
    before, start, guess_in, emit_in, columns, others, out, logscale, token, guess, emit, held, table, row_sems, sems
):
    blocks, states, width = columns.shape
    frames = guess.shape[0]
    first = lax.axis_index("tm") == 0
    core = lax.rem(lax.axis_index("rec"), 2)

    def table_loads(mine):
        copies = []
        for b in range(blocks):
            for k, ref in enumerate((columns, others)):
                at = (2 * b + (mine if k == 0 else 1 - mine)) * width
                copies.append(pltpu.make_async_copy(ref.at[b], table.at[:, pl.ds(at, width)], sems.at[2 * b + k]))
        return copies

    row_loads = [
        pltpu.make_async_copy(guess_in, guess, row_sems.at[0]),
        pltpu.make_async_copy(emit_in, emit, row_sems.at[1]),
    ]
    for copy in row_loads:
        copy.start()
    for mine in range(2):

        @pl.when(core == mine)
        def _():
            for copy in table_loads(mine):
                copy.start()

    for copy in row_loads:
        copy.wait()
    edge = before[...]
    blank = jnp.zeros_like(edge)
    rows = frames + EDGE
    lead = SWEEPS
    prior = jnp.concatenate([blank, pltpu.roll(edge, 3, 0), guess[...].astype(F32)], axis=0)
    prior = pltpu.roll(prior, rows - (EDGE - lead), 0)
    emission = jnp.concatenate([blank, edge, emit[...].astype(F32)], axis=0)
    row = lax.broadcasted_iota(jnp.int32, (rows, 1), 0)
    start_row = start[...].astype(F32)
    held[...] = jnp.where(jnp.logical_and(first, row == lead - 1), start_row, prior).astype(BF16)
    for copy in table_loads(0):
        copy.wait()
    for m in range(1, SWEEPS + 1):
        now = rows if m < SWEEPS else frames
        shifted = pltpu.roll(emission, rows - (EDGE - lead + m), 0)[:now]
        unscaled = []
        for b in range(blocks):
            where = slice(2 * b * width, 2 * (b + 1) * width)
            unscaled.append(matmul(held[:now, :], table[:, where]) * shifted[:, where])
        lanes = sum(u[:, :128] + u[:, 128:] for u in unscaled)
        mean = jnp.sum(lanes, axis=1, keepdims=True) * (1.0 / states)
        inverse = 1.0 / mean
        for b, u in enumerate(unscaled):
            where = slice(2 * b * width, 2 * (b + 1) * width)
            scaled = u * inverse
            if m < SWEEPS:
                fixed = jnp.logical_and(first, row == lead - 1 - m)
                held[:, where] = jnp.where(fixed, start_row[:, where], scaled).astype(BF16)
            else:
                out[:, where] = scaled.astype(BF16)
        if m == SWEEPS:
            logscale[...] = jnp.transpose(jnp.broadcast_to(jnp.log(mean), (frames, 128)))[0:1, :]
    token[...] = jnp.zeros_like(token)


def sweeps(before, guess, emit, start, columns, others):
    frames, states = guess.shape
    return pl.pallas_call(
        sweep_kernel,
        in_specs=[pl.BlockSpec(memory_space=VMEM)] * 2 + [pl.BlockSpec(memory_space=pl.ANY)] * 4,
        out_shape=(
            jax.ShapeDtypeStruct((frames, states), BF16),
            jax.ShapeDtypeStruct((1, frames), F32),
            jax.ShapeDtypeStruct((8, 128), F32),
        ),
        scratch_shapes=[
            VMEM((frames, states), BF16),
            VMEM((frames, states), BF16),
            VMEM((frames + EDGE, states), BF16),
            VMEM((states, states), BF16),
            pltpu.SemaphoreType.DMA((2,)),
            pltpu.SemaphoreType.DMA((2 * columns.shape[0],)),
        ],
        compiler_params=params(),
        cost_estimate=LIGHT,
        name="sweeps",
    )(before, start, guess, emit, columns, others)


def product_kernel(
    own, column_sums, row_sums, before, lower, got, order, out, token, right, left, total, result, load_sems, out_sems
):
    states = own.shape[0]
    parts, depth, _ = right.shape
    half = states // 2
    even = parity() == 0
    token[...] = jnp.zeros_like(token)

    def store(p):
        rows = pl.ds(p * (half // parts), half // parts)
        return pltpu.make_async_copy(result.at[rows, :], out.at[rows, :], out_sems.at[p])

    def finish(scale):
        for p in range(parts):
            rows = slice(p * (half // parts), (p + 1) * (half // parts))
            result[rows, :] = (total[rows, :] * scale).astype(BF16)
            store(p).start()

    @pl.when(even)
    def _():
        loads = [
            pltpu.make_async_copy(got.at[pl.ds(p * depth, depth), :], right.at[p], load_sems.at[p]) for p in range(parts)
        ]
        for load in loads:
            load.start()
        sums = column_sums[...]
        high = sums.astype(BF16).astype(F32)
        mid = (sums - high).astype(BF16).astype(F32)
        row = lax.broadcasted_iota(jnp.int32, (EDGE, states), 0)
        low = sums - high - mid
        split = jnp.where(row == 0, high, jnp.where(row == 1, mid, jnp.where(row == 2, low, 0.0))).astype(BF16)
        for p in range(parts):
            where = slice(p * depth, (p + 1) * depth)
            loads[p].wait()
            block = matmul(jnp.concatenate([own[:half, where], split[:, where]], axis=0), right[p])
            total[...] = block if p == 0 else total[...] + block
        pair = jnp.sum(jnp.sum(total[half:, :], axis=0, keepdims=True), axis=1, keepdims=True)
        finish((states * states) / pair)

    @pl.when(jnp.logical_not(even))
    def _():
        load = pltpu.make_async_copy(lower, left, load_sems.at[0])
        load.start()
        scale = (states * states) / jnp.sum(row_sums[...] * before[0:1], axis=1, keepdims=True)
        load.wait()
        total[:half, :] = matmul(left[...], own[...])
        finish(scale)

    for p in range(parts):
        store(p).wait()


def pair_product(own, column_sums, row_sums, before, lower, got, order):
    states = own.shape[0]
    half, parts = states // 2, 4
    return pl.pallas_call(
        product_kernel,
        in_specs=[pl.BlockSpec(memory_space=VMEM)] * 4 + [pl.BlockSpec(memory_space=pl.ANY)] * 3,
        out_specs=[pl.BlockSpec(memory_space=HBM), pl.BlockSpec(memory_space=VMEM)],
        out_shape=(jax.ShapeDtypeStruct((half, states), BF16), jax.ShapeDtypeStruct((8, 128), F32)),
        scratch_shapes=[
            VMEM((parts, states // parts, states), BF16),
            VMEM((half, states), BF16),
            VMEM((half + EDGE, states), F32),
            VMEM((half, states), BF16),
            pltpu.SemaphoreType.DMA((parts,)),
            pltpu.SemaphoreType.DMA((parts,)),
        ],
        compiler_params=params(),
        cost_estimate=LIGHT,
        name="pair_product",
    )(own, column_sums, row_sums, before, lower, got, order)


def mean_kernel(states, totals, order, level):
    logs = jnp.log(totals[...] * (1.0 / states))
    level[...] = jnp.sum(logs, axis=0, keepdims=True) * (1.0 / logs.shape[0])


def mean_log(totals, states, order):
    return pl.pallas_call(
        functools.partial(mean_kernel, states),
        in_specs=[pl.BlockSpec(memory_space=VMEM), pl.BlockSpec(memory_space=pl.ANY)],
        out_shape=jax.ShapeDtypeStruct((1, 128), F32),
        compiler_params=params(),
        cost_estimate=LIGHT,
        name="mean_log",
    )(totals, order)


def local(summary, guess, emission, transition, start):
    tile = summary[0, 0]
    states = tile.shape[0]
    size, recs = lax.axis_size("tm"), lax.axis_size("rec")
    even = lax.axis_index("tm") % 2 == 0
    back = [(t, t - 1) for t in range(1, size, 2)]
    over = [(t, t + 1) for t in range(0, size, 2)]
    planes = size // 4
    peers = [[r * size + t for t in range(0, size, 2)] for r in range(recs)]
    peers += [[r * size + t for r in range(recs) for t in range(z, size, planes)] for z in range(1, planes, 2)]
    cores = [list(range(c, recs, 2)) for c in range(2)]

    got = lax.ppermute(tile, "tm", back)
    copies = copies_of(transition, recs // 2)
    columns = lax.all_to_all(copies, "rec", 0, 0, tiled=True, axis_index_groups=cores)
    wide = tile.astype(F32)
    column_sums, row_sums = jnp.sum(wide, axis=0)[None], jnp.sum(wide, axis=1)[None]
    edge = make_edge(column_sums, guess[0], emission[0])
    before = lax.ppermute(edge, "tm", [(t, (t + 1) % size) for t in range(size)])
    lower = lax.ppermute(rows_after(tile, states // 2, before), "tm", over)
    total = lax.ppermute(pair_total(before, row_sums), "tm", [(t, (t + 1) % size) for t in range(1, size, 2)])
    totals = spread(total, size // 2)
    totals = lax.all_to_all(totals, ("rec", "tm"), 0, 0, tiled=True, axis_index_groups=peers)
    others = lax.ppermute(columns, "rec", [(r, r ^ 1) for r in range(recs)])
    forward, frame_logscale, token = sweeps(before, guess[0], emission[0], start, columns, others)
    combined, token = pair_product(tile, column_sums, row_sums, before, lower, got, token)
    level = mean_log(totals, states, token)[0, :1]
    told = lax.ppermute(level, "tm", over)
    return combined[None], jnp.where(even, level, told), forward[None], frame_logscale


def solution(mesh):
    return jax.shard_map(
        local,
        mesh=mesh,
        in_specs=(
            P("rec", "tm", None, None),
            P("rec", "tm", None),
            P("rec", "tm", None),
            P(None, "rec"),
            P("rec", None),
        ),
        out_specs=(P("rec", "tm", None), P("rec"), P("rec", "tm", None), P("rec", "tm")),
        check_vma=False,
    )
```
